32 devices in a mesh: aux: 4 (over y, x), row: 8 (over z, core).
Axes of the slice: x: 2, y: 2, z: 4, core: 2. Of those that a mesh axis runs over, the one named last changes fastest.
Arguments:
- coeff: bfloat16 [800, 1024], P(None, 'row'), may hold values from -0.109375 to 0.109375
- band: bfloat16 [8, 384, 1024], P('aux', None, 'row'), may hold values from -6 to 6
- pairs: int32 [8, 8], replicated, may hold values from 0 to 1, as said below
Outputs:
- exchange_k: float32 [1024, 1024], P('row', 'aux')
The draws below stay inside these ranges and needn't reach their ends.
Inputs may be any that keep to these rules, and one draw needn't show every extreme that they name: pairs is symmetric, holds only 0 and 1, and its diagonal is 1; how many blocks a row keeps differs from row to row.
All inputs are finite; a program needn't handle non-finite values.
Results may differ from the reference program's by a relative error of at most 0.0012.
Values may be sent and summed in bfloat16 or wider, within the bound.
A program may use at most 64 MiB of HBM per device.

```python
import jax
import jax.numpy as jnp
from jax import lax

BLK = 128
NOCC = 800
NBLK = 8
NBF = 1024
NAUX = 8


def draw_pairs(key, part):
    key_density, key_ticket = jax.random.split(jax.random.fold_in(key, 7))
    density = jax.random.randint(key_density, (NBLK,), 5, 50)
    ticket = jax.random.randint(key_ticket, (NBLK, NBLK), 0, 100)
    chosen = ticket < density[:, None] + density[None, :]
    positions = jnp.arange(NBLK)
    strict = positions[None, :] > positions[:, None]
    one_side = jnp.where(strict & chosen, 1, 0).astype(jnp.int32)
    return (one_side + one_side.T + jnp.eye(NBLK, dtype=jnp.int32)).astype(jnp.int32)


def shard_levels(key, shape, cuts, least, top_value):
    gain = 1.0
    for position, blocks in cuts:
        heights = jax.random.uniform(jax.random.fold_in(jax.random.fold_in(key, 6), position), (blocks,), jnp.float32, least / len(cuts), top_value / len(cuts))
        gain = gain * jnp.repeat(jnp.exp(heights), shape[position] // blocks).reshape((-1,) + (1,) * (len(shape) - 1 - position))
    return gain


def normal_values(rng, shape, spread, most, cuts=(), kind=jnp.bfloat16):
    level = shard_levels(rng, shape, cuts, -0.22, 0.18) if cuts else 1.0
    result = jax.random.normal(rng, shape, jnp.float32) * spread * level
    return jnp.minimum(jnp.maximum(result, -most), most).astype(kind)


def setup_inputs(seed: int = 0) -> dict:
    keys = jax.random.split(jax.random.key(seed), 4)
    coeff = normal_values(keys[0], (NOCC, NBF), (3 * BLK * 8) ** -0.5, 0.109375, ((1, 8),))
    band = normal_values(keys[1], (NAUX, 3 * BLK, NBF), 1.0, 6.0, ((0, 4), (2, 8)))
    pairs = draw_pairs(jax.random.fold_in(keys[3], 71), 0)
    return dict(coeff=coeff, band=band, pairs=pairs)


def reference(coeff, band, pairs):
    padded = jnp.pad(coeff.astype(jnp.float32), ((0, 0), (BLK, BLK)))
    factors = []
    for block_index in range(NBLK):
        window = padded[:, block_index * BLK:(block_index + 3) * BLK]
        slab_part = band[:, :, block_index * BLK:(block_index + 1) * BLK].astype(jnp.float32)
        product = jnp.einsum("ij,qjm->qim", window, slab_part, precision=lax.Precision.HIGHEST)
        factors.append(product.astype(jnp.bfloat16))
    half_factor = jnp.concatenate(factors, axis=2).reshape(-1, NBF).astype(jnp.float32)
    complete = lax.dot_general(half_factor, half_factor, (((0,), (0,)), ((), ())), precision=lax.Precision.HIGHEST, preferred_element_type=jnp.float32)
    screen = jnp.repeat(jnp.repeat(pairs, BLK, axis=0), BLK, axis=1).astype(jnp.float32)
    return complete * screen
```

```python
import functools

import jax
import jax.numpy as jnp
from jax import lax
from jax.experimental import pallas as pl
from jax.experimental.pallas import tpu as pltpu
from jax.sharding import PartitionSpec as P

MESH = pl.DeviceIdType.MESH


def exchange_kernel(
    rows, groups, coeff_ref, band_ref, pairs_ref, out_ref,
    coeffs, bands, halves, own_t, parts, arrived,
    cz_send, cs_send, ca_send, c_recv, bz_send, bs_send, b_recv, k_send, k_recv,
):
    chips = rows // 2
    occupied, block = coeff_ref.shape
    naux = band_ref.shape[0]
    piece = occupied // 2
    group = lax.axis_index("aux")
    row = lax.axis_index("row")
    chip, core = row // 2, row % 2
    other = chip * 2 + (1 - core)

    def each_side(act):
        for side, step in ((0, 1), (1, -1)):
            target = chip + step
            pl.when((target >= 0) & (target < chips))(
                functools.partial(act, side, target * 2 + core)
            )

    barrier = pltpu.get_barrier_semaphore()

    def greet(side, target):
        pl.semaphore_signal(barrier, inc=1, device_id={"row": target}, device_id_type=MESH)

    each_side(greet)
    pl.semaphore_signal(barrier, inc=1, device_id={"row": other}, device_id_type=MESH)
    for shift in range(1, groups):
        pl.semaphore_signal(
            barrier, inc=1, device_id={"aux": lax.rem(group + shift, groups)}, device_id_type=MESH
        )

    edge = jnp.zeros((occupied, block), coeffs.dtype)
    coeffs[:, :block] = edge
    coeffs[:, (rows + 1) * block:] = edge
    coeffs[:, pl.ds(pl.multiple_of((row + 1) * block, block), block)] = coeff_ref[...]
    bands[row] = band_ref[...]

    sides = jnp.minimum(chip, 1) + jnp.minimum(chips - 1 - chip, 1)
    pl.semaphore_wait(barrier, groups + sides)

    def slot(owner, part):
        return coeffs.at[
            pl.ds(part * piece, piece),
            pl.ds(pl.multiple_of((owner + 1) * block, block), block),
        ]

    def send(src, dst, sent, got, where):
        return pltpu.make_async_remote_copy(
            src_ref=src, dst_ref=dst, send_sem=sent, recv_sem=got,
            device_id=where, device_id_type=MESH,
        )

    def coeff_on(owner, part, side, target):
        return send(slot(owner, part), slot(owner, part), cz_send.at[side, owner, part],
                    c_recv.at[owner, part], {"row": target})

    def coeff_other(owner, part):
        return send(slot(owner, part), slot(owner, part), cs_send.at[owner, part],
                    c_recv.at[owner, part], {"row": other})

    def coeff_aux(owner, part, shift):
        return send(slot(owner, part), slot(owner, part), ca_send.at[owner // 2, part, shift - 1],
                    c_recv.at[owner, part], {"aux": lax.rem(group + shift, groups)})

    def band_on(owner, q, side, target):
        return send(bands.at[owner, q], bands.at[owner, q], bz_send.at[side, owner, q],
                    b_recv.at[owner, q], {"row": target})

    def band_other(owner, q):
        return send(bands.at[owner, q], bands.at[owner, q], bs_send.at[owner, q],
                    b_recv.at[owner, q], {"row": other})

    def carries(owner, part):
        return lax.rem(owner * 2 + part, groups) == group

    def part_out(to):
        return send(parts.at[to], arrived.at[group], k_send.at[to], k_recv.at[group], {"aux": to})

    def start_coeff(side, target):
        for part in range(2):
            pl.when(carries(row, part))(
                lambda part=part: coeff_on(row, part, side, target).start()
            )

    def start_band(side, target):
        for q in range(naux):
            band_on(row, q, side, target).start()

    each_side(start_coeff)
    for part in range(2):
        coeff_other(row, part).start()
    each_side(start_band)
    for q in range(naux):
        band_other(row, q).start()

    def sources(step):
        return ((0, chip - step, chip + 1), (1, chip + step, chip - 1))

    def inside(index):
        return (index >= 0) & (index < chips)

    def relay_coeff(step):
        for side, origin, ahead in sources(step):
            @pl.when(inside(origin))
            def _():
                owner = origin * 2 + core
                for part in range(2):
                    coeff_other(owner, part).wait_recv()

                    @pl.when(carries(owner, part))
                    def _():
                        pl.when(inside(ahead))(
                            lambda: coeff_on(owner, part, side, ahead * 2 + core).start()
                        )
                        for shift in range(1, groups):
                            coeff_aux(owner, part, shift).start()

                    coeff_other(owner, part).start()

    def relay_band(step):
        for side, origin, ahead in sources(step):
            @pl.when(inside(origin))
            def _():
                owner = origin * 2 + core
                for q in range(naux):
                    band_other(owner, q).wait_recv()
                    pl.when(inside(ahead))(
                        lambda: band_on(owner, q, side, ahead * 2 + core).start()
                    )
                    band_other(owner, q).start()

    def other_coeff(step):
        for side, origin, ahead in sources(step):
            @pl.when(inside(origin))
            def _():
                for part in range(2):
                    coeff_other(origin * 2 + 1 - core, part).wait_recv()

    def half_pair(origin):
        for j in range(2):
            owner = origin * 2 + j
            window = coeffs[:, pl.ds(pl.multiple_of(owner * block, block), 3 * block)]
            slab = jnp.concatenate([bands[owner, q] for q in range(naux)], axis=1)
            halves[j] = jnp.dot(window, slab, preferred_element_type=jnp.float32).astype(
                halves.dtype
            )

    def multiply(origin):
        total = None
        for q in range(naux):
            cut = slice(q * block, (q + 1) * block)
            both = jnp.concatenate([halves[0, :, cut], halves[1, :, cut]], axis=1)
            term = jnp.dot(own_t[cut, :], both, preferred_element_type=jnp.float32)
            total = term if total is None else total + term
        parts[origin] = total
        pl.when(origin != group)(lambda: part_out(origin).start())

    relay_coeff(1)
    relay_band(1)
    for part in range(2):
        coeff_other(other, part).wait_recv()
    other_coeff(1)
    for q in range(naux):
        band_other(other, q).wait_recv()
    half_pair(chip)
    own_t[...] = halves[core].T
    multiply(chip)

    def forward(step, carry):
        @pl.when(step + 1 < chips)
        def _():
            relay_coeff(step + 1)
            other_coeff(step + 1)

        for side, origin, ahead in sources(step):
            @pl.when(inside(origin))
            def _():
                for q in range(naux):
                    band_other(origin * 2 + 1 - core, q).wait_recv()
                half_pair(origin)
                multiply(origin)

        pl.when(step + 1 < chips)(lambda: relay_band(step + 1))
        return carry

    lax.fori_loop(1, chips, forward, 0)

    total = parts[group]
    for shift in range(1, groups):
        giver = lax.rem(group + shift, groups)
        send(parts.at[giver], arrived.at[giver], k_send.at[giver], k_recv.at[giver],
             {"aux": giver}).wait_recv()
        total = total + arrived[giver]
    for j in range(2):
        kept = pairs_ref[row, group * 2 + j].astype(jnp.float32)
        out_ref[:, j * block:(j + 1) * block] = total[:, j * block:(j + 1) * block] * kept

    def left_own(side, target):
        for part in range(2):
            pl.when(carries(row, part))(
                lambda part=part: coeff_on(row, part, side, target).wait_send()
            )
        for q in range(naux):
            band_on(row, q, side, target).wait_send()

    each_side(left_own)
    for part in range(2):
        coeff_other(row, part).wait_send()
    for q in range(naux):
        band_other(row, q).wait_send()

    def left(step, carry):
        for side, origin, ahead in sources(step):
            @pl.when(inside(origin))
            def _():
                owner = origin * 2 + core
                for part in range(2):
                    @pl.when(carries(owner, part))
                    def _():
                        pl.when(inside(ahead))(
                            lambda: coeff_on(owner, part, side, ahead * 2 + core).wait_send()
                        )
                        for shift in range(1, groups):
                            coeff_aux(owner, part, shift).wait_send()

                    coeff_other(owner, part).wait_send()
                for q in range(naux):
                    pl.when(inside(ahead))(
                        lambda: band_on(owner, q, side, ahead * 2 + core).wait_send()
                    )
                    band_other(owner, q).wait_send()

        return carry

    lax.fori_loop(1, chips, left, 0)
    for shift in range(1, groups):
        part_out(lax.rem(group + shift, groups)).wait_send()


def on_device(rows, groups, coeff, band, pairs):
    occupied, block = coeff.shape
    naux, depth, _ = band.shape
    chips = rows // 2
    dma = pltpu.SemaphoreType.DMA
    vmem = pl.BlockSpec(memory_space=pltpu.VMEM)
    flops = 2 * rows * naux * occupied * block * (depth + block)
    return pl.pallas_call(
        functools.partial(exchange_kernel, rows, groups),
        out_shape=jax.ShapeDtypeStruct((block, 2 * block), jnp.float32),
        in_specs=[vmem, vmem, pl.BlockSpec(memory_space=pltpu.SMEM)],
        out_specs=vmem,
        scratch_shapes=[
            pltpu.VMEM((occupied, (rows + 2) * block), jnp.bfloat16),
            pltpu.VMEM((rows, naux, depth, block), jnp.bfloat16),
            pltpu.VMEM((2, occupied, naux * block), jnp.bfloat16),
            pltpu.VMEM((naux * block, occupied), jnp.bfloat16),
            pltpu.VMEM((groups, block, 2 * block), jnp.float32),
            pltpu.VMEM((groups, block, 2 * block), jnp.float32),
            dma((2, rows, 2)), dma((rows, 2)), dma((chips, 2, groups - 1)), dma((rows, 2)),
            dma((2, rows, naux)), dma((rows, naux)), dma((rows, naux)),
            dma((groups,)), dma((groups,)),
        ],
        compiler_params=pltpu.CompilerParams(
            collective_id=0, has_side_effects=True, vmem_limit_bytes=48 * 2**20
        ),
        cost_estimate=pl.CostEstimate(flops=flops, bytes_accessed=2**20, transcendentals=0),
    )(coeff, band, pairs)


def solution(mesh):
    rows, groups = mesh.shape["row"], mesh.shape["aux"]
    placed = (P(None, "row"), P("aux", None, "row"), P())
    return jax.shard_map(
        functools.partial(on_device, rows, groups),
        mesh=mesh, in_specs=placed, out_specs=P("row", "aux"), check_vma=False,
    )
```

```python
import functools

import jax
import jax.numpy as jnp
from jax import lax
from jax.experimental import pallas as pl
from jax.experimental.pallas import tpu as pltpu
from jax.sharding import PartitionSpec as P

MESH = pl.DeviceIdType.MESH


def exchange_kernel(
    rows, groups, coeff_ref, band_ref, pairs_ref, out_ref,
    coeffs, bands, halves, own_t, parts, arrived,
    cz_send, cs_send, ca_send, c_recv, bz_send, bs_send, b_recv, k_send, k_recv,
):
    chips = rows // 2
    occupied, block = coeff_ref.shape
    naux = band_ref.shape[0]
    piece = occupied // 2
    group = lax.axis_index("aux")
    row = lax.axis_index("row")
    chip, core = row // 2, row % 2
    other = chip * 2 + (1 - core)

    def each_side(act):
        for side, step in ((0, 1), (1, -1)):
            target = chip + step
            pl.when((target >= 0) & (target < chips))(
                functools.partial(act, side, target * 2 + core)
            )

    barrier = pltpu.get_barrier_semaphore()

    def greet(side, target):
        pl.semaphore_signal(barrier, inc=1, device_id={"row": target}, device_id_type=MESH)

    each_side(greet)
    pl.semaphore_signal(barrier, inc=1, device_id={"row": other}, device_id_type=MESH)
    for shift in range(1, groups):
        pl.semaphore_signal(
            barrier, inc=1, device_id={"aux": lax.rem(group + shift, groups)}, device_id_type=MESH
        )

    edge = jnp.zeros((occupied, block), coeffs.dtype)
    coeffs[0] = edge
    coeffs[rows + 1] = edge
    coeffs[row + 1] = coeff_ref[...]
    bands[row] = band_ref[...]

    sides = jnp.minimum(chip, 1) + jnp.minimum(chips - 1 - chip, 1)
    pl.semaphore_wait(barrier, groups + sides)

    def slot(owner, part):
        return coeffs.at[owner + 1, pl.ds(part * piece, piece)]

    def send(src, dst, sent, got, where):
        return pltpu.make_async_remote_copy(
            src_ref=src, dst_ref=dst, send_sem=sent, recv_sem=got,
            device_id=where, device_id_type=MESH,
        )

    def coeff_on(owner, part, side, target):
        return send(slot(owner, part), slot(owner, part), cz_send.at[side, owner, part],
                    c_recv.at[owner, part], {"row": target})

    def coeff_other(owner, part):
        return send(slot(owner, part), slot(owner, part), cs_send.at[owner, part],
                    c_recv.at[owner, part], {"row": other})

    def coeff_aux(owner, part, shift):
        return send(slot(owner, part), slot(owner, part), ca_send.at[owner // 2, part, shift - 1],
                    c_recv.at[owner, part], {"aux": lax.rem(group + shift, groups)})

    def band_on(owner, q, side, target):
        return send(bands.at[owner, q], bands.at[owner, q], bz_send.at[side, owner, q],
                    b_recv.at[owner, q], {"row": target})

    def band_other(owner, q):
        return send(bands.at[owner, q], bands.at[owner, q], bs_send.at[owner, q],
                    b_recv.at[owner, q], {"row": other})

    def carries(owner, part):
        return lax.rem(owner * 2 + part, groups) == group

    def part_out(to):
        return send(parts.at[to], arrived.at[group], k_send.at[to], k_recv.at[group], {"aux": to})

    def start_coeff(side, target):
        for part in range(2):
            pl.when(carries(row, part))(
                lambda part=part: coeff_on(row, part, side, target).start()
            )

    def start_band(side, target):
        for q in range(naux):
            band_on(row, q, side, target).start()

    each_side(start_coeff)
    for part in range(2):
        coeff_other(row, part).start()
    each_side(start_band)
    for q in range(naux):
        band_other(row, q).start()

    def sources(step):
        return ((0, chip - step, chip + 1), (1, chip + step, chip - 1))

    def inside(index):
        return (index >= 0) & (index < chips)

    def relay_row(step):
        for side, origin, ahead in sources(step):
            @pl.when(inside(origin))
            def _():
                owner = origin * 2 + core
                for part in range(2):
                    @pl.when(carries(owner, part))
                    def _():
                        coeff_other(owner, part).wait_recv()
                        pl.when(inside(ahead))(
                            lambda: coeff_on(owner, part, side, ahead * 2 + core).start()
                        )
                        for shift in range(1, groups):
                            coeff_aux(owner, part, shift).start()
                        coeff_other(owner, part).start()

        for side, origin, ahead in sources(step):
            @pl.when(inside(origin))
            def _():
                owner = origin * 2 + core
                for q in range(naux):
                    band_other(owner, q).wait_recv()
                    pl.when(inside(ahead))(
                        lambda: band_on(owner, q, side, ahead * 2 + core).start()
                    )
                    band_other(owner, q).start()

    def relay_groups(step):
        for side, origin, ahead in sources(step):
            @pl.when(inside(origin))
            def _():
                owner = origin * 2 + core
                for part in range(2):
                    @pl.when(jnp.logical_not(carries(owner, part)))
                    def _():
                        coeff_other(owner, part).wait_recv()
                        coeff_other(owner, part).start()

        for side, origin, ahead in sources(step):
            @pl.when(inside(origin))
            def _():
                for part in range(2):
                    coeff_other(origin * 2 + 1 - core, part).wait_recv()

    def half_pair(origin):
        for j in range(2):
            owner = origin * 2 + j
            window = jnp.concatenate([coeffs[owner + near] for near in range(3)], axis=1)
            slab = jnp.concatenate([bands[owner, q] for q in range(naux)], axis=1)
            halves[j] = jnp.dot(window, slab, preferred_element_type=jnp.float32).astype(
                halves.dtype
            )

    def multiply(origin):
        total = None
        for q in range(naux):
            cut = slice(q * block, (q + 1) * block)
            both = jnp.concatenate([halves[0, :, cut], halves[1, :, cut]], axis=1)
            term = jnp.dot(own_t[cut, :], both, preferred_element_type=jnp.float32)
            total = term if total is None else total + term
        parts[origin] = total
        pl.when(origin != group)(lambda: part_out(origin).start())

    for step in range(1, min(chips, 3)):
        relay_row(step)
    for part in range(2):
        coeff_other(other, part).wait_recv()
    relay_groups(1)
    for q in range(naux):
        band_other(other, q).wait_recv()
    half_pair(chip)
    own_t[...] = halves[core].T
    multiply(chip)

    def forward(step, carry):
        pl.when(step + 2 < chips)(lambda: relay_row(step + 2))
        pl.when(step + 1 < chips)(lambda: relay_groups(step + 1))

        for side, origin, ahead in sources(step):
            @pl.when(inside(origin))
            def _():
                for q in range(naux):
                    band_other(origin * 2 + 1 - core, q).wait_recv()
                half_pair(origin)
                multiply(origin)

        return carry

    lax.fori_loop(1, chips, forward, 0)

    total = parts[group]
    for shift in range(1, groups):
        giver = lax.rem(group + shift, groups)
        send(parts.at[giver], arrived.at[giver], k_send.at[giver], k_recv.at[giver],
             {"aux": giver}).wait_recv()
        total = total + arrived[giver]
    for j in range(2):
        kept = pairs_ref[row, group * 2 + j].astype(jnp.float32)
        out_ref[:, j * block:(j + 1) * block] = total[:, j * block:(j + 1) * block] * kept

    def left_own(side, target):
        for part in range(2):
            pl.when(carries(row, part))(
                lambda part=part: coeff_on(row, part, side, target).wait_send()
            )
        for q in range(naux):
            band_on(row, q, side, target).wait_send()

    each_side(left_own)
    for part in range(2):
        coeff_other(row, part).wait_send()
    for q in range(naux):
        band_other(row, q).wait_send()

    def left(step, carry):
        for side, origin, ahead in sources(step):
            @pl.when(inside(origin))
            def _():
                owner = origin * 2 + core
                for part in range(2):
                    @pl.when(carries(owner, part))
                    def _():
                        pl.when(inside(ahead))(
                            lambda: coeff_on(owner, part, side, ahead * 2 + core).wait_send()
                        )
                        for shift in range(1, groups):
                            coeff_aux(owner, part, shift).wait_send()

                    coeff_other(owner, part).wait_send()
                for q in range(naux):
                    pl.when(inside(ahead))(
                        lambda: band_on(owner, q, side, ahead * 2 + core).wait_send()
                    )
                    band_other(owner, q).wait_send()

        return carry

    lax.fori_loop(1, chips, left, 0)
    for shift in range(1, groups):
        part_out(lax.rem(group + shift, groups)).wait_send()


def on_device(rows, groups, coeff, band, pairs):
    occupied, block = coeff.shape
    naux, depth, _ = band.shape
    chips = rows // 2
    dma = pltpu.SemaphoreType.DMA
    vmem = pl.BlockSpec(memory_space=pltpu.VMEM)
    flops = 2 * rows * naux * occupied * block * (depth + block)
    return pl.pallas_call(
        functools.partial(exchange_kernel, rows, groups),
        out_shape=jax.ShapeDtypeStruct((block, 2 * block), jnp.float32),
        in_specs=[vmem, vmem, pl.BlockSpec(memory_space=pltpu.SMEM)],
        out_specs=vmem,
        scratch_shapes=[
            pltpu.VMEM((rows + 2, occupied, block), jnp.bfloat16),
            pltpu.VMEM((rows, naux, depth, block), jnp.bfloat16),
            pltpu.VMEM((2, occupied, naux * block), jnp.bfloat16),
            pltpu.VMEM((naux * block, occupied), jnp.bfloat16),
            pltpu.VMEM((groups, block, 2 * block), jnp.float32),
            pltpu.VMEM((groups, block, 2 * block), jnp.float32),
            dma((2, rows, 2)), dma((rows, 2)), dma((chips, 2, groups - 1)), dma((rows, 2)),
            dma((2, rows, naux)), dma((rows, naux)), dma((rows, naux)),
            dma((groups,)), dma((groups,)),
        ],
        compiler_params=pltpu.CompilerParams(
            collective_id=0, has_side_effects=True, vmem_limit_bytes=48 * 2**20
        ),
        cost_estimate=pl.CostEstimate(flops=flops, bytes_accessed=2**20, transcendentals=0),
    )(coeff, band, pairs)


def solution(mesh):
    rows, groups = mesh.shape["row"], mesh.shape["aux"]
    placed = (P(None, "row"), P("aux", None, "row"), P())
    return jax.shard_map(
        functools.partial(on_device, rows, groups),
        mesh=mesh, in_specs=placed, out_specs=P("row", "aux"), check_vma=False,
    )
```

```python
import functools

import jax
import jax.numpy as jnp
from jax import lax
from jax.experimental import pallas as pl
from jax.experimental.pallas import tpu as pltpu
from jax.sharding import PartitionSpec as P

MESH = pl.DeviceIdType.MESH


def exchange_kernel(
    rows, groups, coeff_ref, band_ref, pairs_ref, out_ref,
    coeffs, bands, halves, own_t, parts, arrived,
    cz_send, cs_send, ca_send, c_recv, bz_send, bs_send, b_recv, k_send, k_recv,
    own_sem,
):
    chips = rows // 2
    occupied, block = coeff_ref.shape
    naux = band_ref.shape[0]
    piece = occupied // 2
    group = lax.axis_index("aux")
    row = lax.axis_index("row")
    chip, core = row // 2, row % 2
    other = chip * 2 + (1 - core)

    def each_side(act):
        for side, step in ((0, 1), (1, -1)):
            target = chip + step
            pl.when((target >= 0) & (target < chips))(
                functools.partial(act, side, target * 2 + core)
            )

    barrier = pltpu.get_barrier_semaphore()

    def greet(side, target):
        pl.semaphore_signal(barrier, inc=1, device_id={"row": target}, device_id_type=MESH)

    each_side(greet)
    pl.semaphore_signal(barrier, inc=1, device_id={"row": other}, device_id_type=MESH)
    for shift in range(1, groups):
        pl.semaphore_signal(
            barrier, inc=1, device_id={"aux": lax.rem(group + shift, groups)}, device_id_type=MESH
        )

    own_coeff = pltpu.make_async_copy(coeff_ref, coeffs.at[row + 1], own_sem.at[0])
    own_band = pltpu.make_async_copy(band_ref, bands.at[row], own_sem.at[1])
    own_coeff.start()
    own_band.start()
    edge = jnp.zeros((occupied, block), coeffs.dtype)
    coeffs[0] = edge
    coeffs[rows + 1] = edge

    sides = jnp.minimum(chip, 1) + jnp.minimum(chips - 1 - chip, 1)
    pl.semaphore_wait(barrier, groups + sides)

    def slot(owner, part):
        return coeffs.at[owner + 1, pl.ds(part * piece, piece)]

    def send(src, dst, sent, got, where):
        return pltpu.make_async_remote_copy(
            src_ref=src, dst_ref=dst, send_sem=sent, recv_sem=got,
            device_id=where, device_id_type=MESH,
        )

    def coeff_on(owner, part, side, target):
        return send(slot(owner, part), slot(owner, part), cz_send.at[side, owner, part],
                    c_recv.at[owner, part], {"row": target})

    def coeff_other(owner, part):
        return send(slot(owner, part), slot(owner, part), cs_send.at[owner, part],
                    c_recv.at[owner, part], {"row": other})

    def coeff_aux(owner, part, shift):
        return send(slot(owner, part), slot(owner, part), ca_send.at[owner // 2, part, shift - 1],
                    c_recv.at[owner, part], {"aux": lax.rem(group + shift, groups)})

    def band_on(owner, q, side, target):
        return send(bands.at[owner, q], bands.at[owner, q], bz_send.at[side, owner, q],
                    b_recv.at[owner, q], {"row": target})

    def band_other(owner, q):
        return send(bands.at[owner, q], bands.at[owner, q], bs_send.at[owner, q],
                    b_recv.at[owner, q], {"row": other})

    def carries(owner, part):
        return lax.rem(owner * 2 + part, groups) == group

    def part_out(to):
        return send(parts.at[to], arrived.at[group], k_send.at[to], k_recv.at[group], {"aux": to})

    def start_coeff(side, target):
        for part in range(2):
            pl.when(carries(row, part))(
                lambda part=part: coeff_on(row, part, side, target).start()
            )

    def start_band(side, target):
        for q in range(naux):
            band_on(row, q, side, target).start()

    own_coeff.wait()
    each_side(start_coeff)
    for part in range(2):
        coeff_other(row, part).start()
    own_band.wait()
    each_side(start_band)
    for q in range(naux):
        band_other(row, q).start()

    def sources(step):
        return ((0, chip - step, chip + 1), (1, chip + step, chip - 1))

    def inside(index):
        return (index >= 0) & (index < chips)

    def relay_row(step):
        for side, origin, ahead in sources(step):
            @pl.when(inside(origin))
            def _():
                owner = origin * 2 + core
                for part in range(2):
                    @pl.when(carries(owner, part))
                    def _():
                        coeff_other(owner, part).wait_recv()
                        pl.when(inside(ahead))(
                            lambda: coeff_on(owner, part, side, ahead * 2 + core).start()
                        )
                        for shift in range(1, groups):
                            coeff_aux(owner, part, shift).start()
                        coeff_other(owner, part).start()

        for side, origin, ahead in sources(step):
            @pl.when(inside(origin))
            def _():
                owner = origin * 2 + core
                for q in range(naux):
                    band_other(owner, q).wait_recv()
                    pl.when(inside(ahead))(
                        lambda: band_on(owner, q, side, ahead * 2 + core).start()
                    )
                    band_other(owner, q).start()

    def relay_groups(step):
        for side, origin, ahead in sources(step):
            @pl.when(inside(origin))
            def _():
                owner = origin * 2 + core
                for part in range(2):
                    @pl.when(jnp.logical_not(carries(owner, part)))
                    def _():
                        coeff_other(owner, part).wait_recv()
                        coeff_other(owner, part).start()

        for side, origin, ahead in sources(step):
            @pl.when(inside(origin))
            def _():
                for part in range(2):
                    coeff_other(origin * 2 + 1 - core, part).wait_recv()

    def half_pair(origin):
        for j in range(2):
            owner = origin * 2 + j
            window = jnp.concatenate([coeffs[owner + near] for near in range(3)], axis=1)
            slab = jnp.concatenate([bands[owner, q] for q in range(naux)], axis=1)
            halves[j] = jnp.dot(window, slab, preferred_element_type=jnp.float32).astype(
                halves.dtype
            )

    def multiply(origin):
        total = None
        for q in range(naux):
            cut = slice(q * block, (q + 1) * block)
            both = jnp.concatenate([halves[0, :, cut], halves[1, :, cut]], axis=1)
            term = jnp.dot(own_t[cut, :], both, preferred_element_type=jnp.float32)
            total = term if total is None else total + term
        parts[origin] = total
        pl.when(origin != group)(lambda: part_out(origin).start())

    for step in range(1, min(chips, 4)):
        relay_row(step)
    for part in range(2):
        coeff_other(other, part).wait_recv()
    relay_groups(1)
    for q in range(naux):
        band_other(other, q).wait_recv()
    half_pair(chip)
    own_t[...] = halves[core].T
    multiply(chip)

    def forward(step, carry):
        pl.when(step + 3 < chips)(lambda: relay_row(step + 3))
        pl.when(step + 1 < chips)(lambda: relay_groups(step + 1))

        for side, origin, ahead in sources(step):
            @pl.when(inside(origin))
            def _():
                for q in range(naux):
                    band_other(origin * 2 + 1 - core, q).wait_recv()
                half_pair(origin)
                multiply(origin)

        return carry

    lax.fori_loop(1, chips, forward, 0)

    total = parts[group]
    for shift in range(1, groups):
        giver = lax.rem(group + shift, groups)
        send(parts.at[giver], arrived.at[giver], k_send.at[giver], k_recv.at[giver],
             {"aux": giver}).wait_recv()
        total = total + arrived[giver]
    for j in range(2):
        kept = pairs_ref[row, group * 2 + j].astype(jnp.float32)
        out_ref[:, j * block:(j + 1) * block] = total[:, j * block:(j + 1) * block] * kept

    def left_own(side, target):
        for part in range(2):
            pl.when(carries(row, part))(
                lambda part=part: coeff_on(row, part, side, target).wait_send()
            )
        for q in range(naux):
            band_on(row, q, side, target).wait_send()

    each_side(left_own)
    for part in range(2):
        coeff_other(row, part).wait_send()
    for q in range(naux):
        band_other(row, q).wait_send()

    def left(step, carry):
        for side, origin, ahead in sources(step):
            @pl.when(inside(origin))
            def _():
                owner = origin * 2 + core
                for part in range(2):
                    @pl.when(carries(owner, part))
                    def _():
                        pl.when(inside(ahead))(
                            lambda: coeff_on(owner, part, side, ahead * 2 + core).wait_send()
                        )
                        for shift in range(1, groups):
                            coeff_aux(owner, part, shift).wait_send()

                    coeff_other(owner, part).wait_send()
                for q in range(naux):
                    pl.when(inside(ahead))(
                        lambda: band_on(owner, q, side, ahead * 2 + core).wait_send()
                    )
                    band_other(owner, q).wait_send()

        return carry

    lax.fori_loop(1, chips, left, 0)
    for shift in range(1, groups):
        part_out(lax.rem(group + shift, groups)).wait_send()


def on_device(rows, groups, coeff, band, pairs):
    occupied, block = coeff.shape
    naux, depth, _ = band.shape
    chips = rows // 2
    dma = pltpu.SemaphoreType.DMA
    held = pl.BlockSpec(memory_space=pl.ANY)
    vmem = pl.BlockSpec(memory_space=pltpu.VMEM)
    flops = 2 * rows * naux * occupied * block * (depth + block)
    return pl.pallas_call(
        functools.partial(exchange_kernel, rows, groups),
        out_shape=jax.ShapeDtypeStruct((block, 2 * block), jnp.float32),
        in_specs=[held, held, pl.BlockSpec(memory_space=pltpu.SMEM)],
        out_specs=vmem,
        scratch_shapes=[
            pltpu.VMEM((rows + 2, occupied, block), jnp.bfloat16),
            pltpu.VMEM((rows, naux, depth, block), jnp.bfloat16),
            pltpu.VMEM((2, occupied, naux * block), jnp.bfloat16),
            pltpu.VMEM((naux * block, occupied), jnp.bfloat16),
            pltpu.VMEM((groups, block, 2 * block), jnp.float32),
            pltpu.VMEM((groups, block, 2 * block), jnp.float32),
            dma((2, rows, 2)), dma((rows, 2)), dma((chips, 2, groups - 1)), dma((rows, 2)),
            dma((2, rows, naux)), dma((rows, naux)), dma((rows, naux)),
            dma((groups,)), dma((groups,)), dma((2,)),
        ],
        compiler_params=pltpu.CompilerParams(
            collective_id=0, has_side_effects=True, vmem_limit_bytes=48 * 2**20
        ),
        cost_estimate=pl.CostEstimate(flops=flops, bytes_accessed=2**20, transcendentals=0),
    )(coeff, band, pairs)


def solution(mesh):
    rows, groups = mesh.shape["row"], mesh.shape["aux"]
    placed = (P(None, "row"), P("aux", None, "row"), P())
    return jax.shard_map(
        functools.partial(on_device, rows, groups),
        mesh=mesh, in_specs=placed, out_specs=P("row", "aux"), check_vma=False,
    )
```

```python
import functools

import jax
import jax.numpy as jnp
from jax import lax
from jax.experimental import pallas as pl
from jax.experimental.pallas import tpu as pltpu
from jax.sharding import PartitionSpec as P

MESH = pl.DeviceIdType.MESH


def exchange_kernel(
    rows, groups, coeff_ref, band_ref, pairs_ref, out_ref,
    coeffs, bands, halves, own_t, parts, arrived,
    cz_send, cs_send, ca_send, c_recv, bz_send, bs_send, b_recv, k_send, k_recv,
    own_sem,
):
    chips = rows // 2
    occupied, block = coeff_ref.shape
    naux = band_ref.shape[0]
    piece = occupied // 2
    group = lax.axis_index("aux")
    row = lax.axis_index("row")
    chip, core = row // 2, row % 2
    other = chip * 2 + (1 - core)

    def each_side(act):
        for side, step in ((0, 1), (1, -1)):
            target = chip + step
            pl.when((target >= 0) & (target < chips))(
                functools.partial(act, side, target * 2 + core)
            )

    barrier = pltpu.get_barrier_semaphore()

    def greet(side, target):
        pl.semaphore_signal(barrier, inc=1, device_id={"row": target}, device_id_type=MESH)

    each_side(greet)
    pl.semaphore_signal(barrier, inc=1, device_id={"row": other}, device_id_type=MESH)
    for shift in range(1, groups):
        pl.semaphore_signal(
            barrier, inc=1, device_id={"aux": lax.rem(group + shift, groups)}, device_id_type=MESH
        )

    own_coeff = pltpu.make_async_copy(coeff_ref, coeffs.at[row + 1], own_sem.at[0])
    own_band = pltpu.make_async_copy(band_ref, bands.at[row], own_sem.at[1])
    own_coeff.start()
    own_band.start()
    edge = jnp.zeros((occupied, block), coeffs.dtype)
    coeffs[0] = edge
    coeffs[rows + 1] = edge

    sides = jnp.minimum(chip, 1) + jnp.minimum(chips - 1 - chip, 1)
    pl.semaphore_wait(barrier, groups + sides)

    def slot(owner, part):
        return coeffs.at[owner + 1, pl.ds(part * piece, piece)]

    def send(src, dst, sent, got, where):
        return pltpu.make_async_remote_copy(
            src_ref=src, dst_ref=dst, send_sem=sent, recv_sem=got,
            device_id=where, device_id_type=MESH,
        )

    def coeff_on(owner, part, side, target):
        return send(slot(owner, part), slot(owner, part), cz_send.at[side, owner, part],
                    c_recv.at[owner, part], {"row": target})

    def coeff_other(owner, part):
        return send(slot(owner, part), slot(owner, part), cs_send.at[owner, part],
                    c_recv.at[owner, part], {"row": other})

    def coeff_aux(owner, part, shift):
        return send(slot(owner, part), slot(owner, part), ca_send.at[owner // 2, part, shift - 1],
                    c_recv.at[owner, part], {"aux": lax.rem(group + shift, groups)})

    def band_on(owner, q, side, target):
        return send(bands.at[owner, q], bands.at[owner, q], bz_send.at[side, owner, q],
                    b_recv.at[owner, q], {"row": target})

    def band_other(owner, q):
        return send(bands.at[owner, q], bands.at[owner, q], bs_send.at[owner, q],
                    b_recv.at[owner, q], {"row": other})

    def carries(owner, part):
        return lax.rem(owner * 2 + part, groups) == group

    def part_out(to):
        return send(parts.at[to], arrived.at[group], k_send.at[to], k_recv.at[group], {"aux": to})

    def start_coeff(side, target):
        for part in range(2):
            pl.when(carries(row, part))(
                lambda part=part: coeff_on(row, part, side, target).start()
            )

    def start_band(side, target):
        for q in range(naux):
            band_on(row, q, side, target).start()

    own_coeff.wait()
    each_side(start_coeff)
    for part in range(2):
        coeff_other(row, part).start()
    own_band.wait()
    each_side(start_band)
    for q in range(naux):
        band_other(row, q).start()

    def sources(step):
        return ((0, chip - step, chip + 1), (1, chip + step, chip - 1))

    def inside(index):
        return (index >= 0) & (index < chips)

    def relay_row(step):
        for side, origin, ahead in sources(step):
            @pl.when(inside(origin))
            def _():
                owner = origin * 2 + core
                for part in range(2):
                    @pl.when(carries(owner, part))
                    def _():
                        coeff_other(owner, part).wait_recv()
                        pl.when(inside(ahead))(
                            lambda: coeff_on(owner, part, side, ahead * 2 + core).start()
                        )
                        for shift in range(1, groups):
                            coeff_aux(owner, part, shift).start()
                        coeff_other(owner, part).start()

        for side, origin, ahead in sources(step):
            @pl.when(inside(origin))
            def _():
                owner = origin * 2 + core
                for q in range(naux):
                    band_other(owner, q).wait_recv()
                    pl.when(inside(ahead))(
                        lambda: band_on(owner, q, side, ahead * 2 + core).start()
                    )
                    band_other(owner, q).start()

    def relay_groups(step):
        for side, origin, ahead in sources(step):
            @pl.when(inside(origin))
            def _():
                owner = origin * 2 + core
                for part in range(2):
                    @pl.when(jnp.logical_not(carries(owner, part)))
                    def _():
                        coeff_other(owner, part).wait_recv()
                        coeff_other(owner, part).start()

        for side, origin, ahead in sources(step):
            @pl.when(inside(origin))
            def _():
                for part in range(2):
                    coeff_other(origin * 2 + 1 - core, part).wait_recv()

    def half_pair(origin):
        for j in range(2):
            owner = origin * 2 + j
            window = jnp.concatenate([coeffs[owner + near] for near in range(3)], axis=1)
            slab = jnp.concatenate([bands[owner, q] for q in range(naux)], axis=1)
            halves[j] = jnp.dot(window, slab, preferred_element_type=jnp.float32).astype(
                halves.dtype
            )

    def multiply(origin):
        total = None
        for q in range(naux):
            cut = slice(q * block, (q + 1) * block)
            both = jnp.concatenate([halves[0, :, cut], halves[1, :, cut]], axis=1)
            term = jnp.dot(own_t[cut, :], both, preferred_element_type=jnp.float32)
            total = term if total is None else total + term
        parts[origin] = total
        pl.when(origin != group)(lambda: part_out(origin).start())

    relay_row(1)
    for part in range(2):
        coeff_other(other, part).wait_recv()
    for q in range(naux):
        band_other(other, q).wait_recv()
    if chips > 2:
        relay_row(2)
    relay_groups(1)
    half_pair(chip)
    if chips > 3:
        relay_row(3)
    own_t[...] = halves[core].T
    multiply(chip)

    def forward(step, carry):
        pl.when(step + 3 < chips)(lambda: relay_row(step + 3))
        pl.when(step + 1 < chips)(lambda: relay_groups(step + 1))

        for side, origin, ahead in sources(step):
            @pl.when(inside(origin))
            def _():
                for q in range(naux):
                    band_other(origin * 2 + 1 - core, q).wait_recv()
                half_pair(origin)
                multiply(origin)

        return carry

    lax.fori_loop(1, chips, forward, 0)

    total = parts[group]
    for shift in range(1, groups):
        giver = lax.rem(group + shift, groups)
        send(parts.at[giver], arrived.at[giver], k_send.at[giver], k_recv.at[giver],
             {"aux": giver}).wait_recv()
        total = total + arrived[giver]
    for j in range(2):
        kept = pairs_ref[row, group * 2 + j].astype(jnp.float32)
        out_ref[:, j * block:(j + 1) * block] = total[:, j * block:(j + 1) * block] * kept

    def left_own(side, target):
        for part in range(2):
            pl.when(carries(row, part))(
                lambda part=part: coeff_on(row, part, side, target).wait_send()
            )
        for q in range(naux):
            band_on(row, q, side, target).wait_send()

    each_side(left_own)
    for part in range(2):
        coeff_other(row, part).wait_send()
    for q in range(naux):
        band_other(row, q).wait_send()

    def left(step, carry):
        for side, origin, ahead in sources(step):
            @pl.when(inside(origin))
            def _():
                owner = origin * 2 + core
                for part in range(2):
                    @pl.when(carries(owner, part))
                    def _():
                        pl.when(inside(ahead))(
                            lambda: coeff_on(owner, part, side, ahead * 2 + core).wait_send()
                        )
                        for shift in range(1, groups):
                            coeff_aux(owner, part, shift).wait_send()

                    coeff_other(owner, part).wait_send()
                for q in range(naux):
                    pl.when(inside(ahead))(
                        lambda: band_on(owner, q, side, ahead * 2 + core).wait_send()
                    )
                    band_other(owner, q).wait_send()

        return carry

    lax.fori_loop(1, chips, left, 0)
    for shift in range(1, groups):
        part_out(lax.rem(group + shift, groups)).wait_send()


def on_device(rows, groups, coeff, band, pairs):
    occupied, block = coeff.shape
    naux, depth, _ = band.shape
    chips = rows // 2
    dma = pltpu.SemaphoreType.DMA
    held = pl.BlockSpec(memory_space=pl.ANY)
    vmem = pl.BlockSpec(memory_space=pltpu.VMEM)
    flops = 2 * rows * naux * occupied * block * (depth + block)
    return pl.pallas_call(
        functools.partial(exchange_kernel, rows, groups),
        out_shape=jax.ShapeDtypeStruct((block, 2 * block), jnp.float32),
        in_specs=[held, held, pl.BlockSpec(memory_space=pltpu.SMEM)],
        out_specs=vmem,
        scratch_shapes=[
            pltpu.VMEM((rows + 2, occupied, block), jnp.bfloat16),
            pltpu.VMEM((rows, naux, depth, block), jnp.bfloat16),
            pltpu.VMEM((2, occupied, naux * block), jnp.bfloat16),
            pltpu.VMEM((naux * block, occupied), jnp.bfloat16),
            pltpu.VMEM((groups, block, 2 * block), jnp.float32),
            pltpu.VMEM((groups, block, 2 * block), jnp.float32),
            dma((2, rows, 2)), dma((rows, 2)), dma((chips, 2, groups - 1)), dma((rows, 2)),
            dma((2, rows, naux)), dma((rows, naux)), dma((rows, naux)),
            dma((groups,)), dma((groups,)), dma((2,)),
        ],
        compiler_params=pltpu.CompilerParams(
            collective_id=0, has_side_effects=True, vmem_limit_bytes=48 * 2**20
        ),
        cost_estimate=pl.CostEstimate(flops=flops, bytes_accessed=2**20, transcendentals=0),
    )(coeff, band, pairs)


def solution(mesh):
    rows, groups = mesh.shape["row"], mesh.shape["aux"]
    placed = (P(None, "row"), P("aux", None, "row"), P())
    return jax.shard_map(
        functools.partial(on_device, rows, groups),
        mesh=mesh, in_specs=placed, out_specs=P("row", "aux"), check_vma=False,
    )
```

```python
import functools

import jax
import jax.numpy as jnp
from jax import lax
from jax.experimental import pallas as pl
from jax.experimental.pallas import tpu as pltpu
from jax.sharding import PartitionSpec as P

MESH = pl.DeviceIdType.MESH


def exchange_kernel(
    rows, groups, coeff_ref, band_ref, pairs_ref, out_ref,
    coeffs, bands, halves, own_t, parts, arrived,
    cz_send, cs_send, ca_send, c_recv, bz_send, bs_send, b_recv, k_send, k_recv,
    own_sem, kept_pairs,
):
    chips = rows // 2
    occupied, block = coeff_ref.shape
    naux = band_ref.shape[0]
    piece = occupied // 2
    group = lax.axis_index("aux")
    row = lax.axis_index("row")
    chip, core = row // 2, row % 2
    other = chip * 2 + (1 - core)

    def each_side(act):
        for side, step in ((0, 1), (1, -1)):
            target = chip + step
            pl.when((target >= 0) & (target < chips))(
                functools.partial(act, side, target * 2 + core)
            )

    barrier = pltpu.get_barrier_semaphore()

    def greet(side, target):
        pl.semaphore_signal(barrier, inc=1, device_id={"row": target}, device_id_type=MESH)

    each_side(greet)
    pl.semaphore_signal(barrier, inc=1, device_id={"row": other}, device_id_type=MESH)
    for shift in range(1, groups):
        pl.semaphore_signal(
            barrier, inc=1, device_id={"aux": lax.rem(group + shift, groups)}, device_id_type=MESH
        )

    own_coeff = pltpu.make_async_copy(coeff_ref, coeffs.at[row + 1], own_sem.at[0])
    own_band = pltpu.make_async_copy(band_ref, bands.at[row], own_sem.at[1])
    own_coeff.start()
    own_band.start()
    own_pairs = pltpu.make_async_copy(pairs_ref, kept_pairs, own_sem.at[2])
    own_pairs.start()
    edge = jnp.zeros((occupied, block), coeffs.dtype)
    coeffs[0] = edge
    coeffs[rows + 1] = edge

    sides = jnp.minimum(chip, 1) + jnp.minimum(chips - 1 - chip, 1)
    pl.semaphore_wait(barrier, groups + sides)

    def slot(owner, part):
        return coeffs.at[owner + 1, pl.ds(part * piece, piece)]

    def send(src, dst, sent, got, where):
        return pltpu.make_async_remote_copy(
            src_ref=src, dst_ref=dst, send_sem=sent, recv_sem=got,
            device_id=where, device_id_type=MESH,
        )

    def coeff_on(owner, part, side, target):
        return send(slot(owner, part), slot(owner, part), cz_send.at[side, owner, part],
                    c_recv.at[owner, part], {"row": target})

    def coeff_other(owner, part):
        return send(slot(owner, part), slot(owner, part), cs_send.at[owner, part],
                    c_recv.at[owner, part], {"row": other})

    def coeff_aux(owner, part, shift):
        return send(slot(owner, part), slot(owner, part), ca_send.at[owner // 2, part, shift - 1],
                    c_recv.at[owner, part], {"aux": lax.rem(group + shift, groups)})

    def band_on(owner, q, side, target):
        return send(bands.at[owner, q], bands.at[owner, q], bz_send.at[side, owner, q],
                    b_recv.at[owner, q], {"row": target})

    def band_other(owner, q):
        return send(bands.at[owner, q], bands.at[owner, q], bs_send.at[owner, q],
                    b_recv.at[owner, q], {"row": other})

    def carries(owner, part):
        return lax.rem(owner * 2 + part, groups) == group

    def part_out(to):
        return send(parts.at[to], arrived.at[group], k_send.at[to], k_recv.at[group], {"aux": to})

    def start_coeff(side, target):
        for part in range(2):
            pl.when(carries(row, part))(
                lambda part=part: coeff_on(row, part, side, target).start()
            )

    def start_band(side, target):
        for q in range(naux):
            band_on(row, q, side, target).start()

    own_coeff.wait()
    each_side(start_coeff)
    for part in range(2):
        coeff_other(row, part).start()
    own_band.wait()
    each_side(start_band)
    for q in range(naux):
        band_other(row, q).start()
    own_pairs.wait()

    def sources(step):
        return ((0, chip - step, chip + 1), (1, chip + step, chip - 1))

    def inside(index):
        return (index >= 0) & (index < chips)

    def relay_row(step):
        for side, origin, ahead in sources(step):
            @pl.when(inside(origin))
            def _():
                owner = origin * 2 + core
                for part in range(2):
                    @pl.when(carries(owner, part))
                    def _():
                        coeff_other(owner, part).wait_recv()
                        pl.when(inside(ahead))(
                            lambda: coeff_on(owner, part, side, ahead * 2 + core).start()
                        )
                        for shift in range(1, groups):
                            coeff_aux(owner, part, shift).start()
                        coeff_other(owner, part).start()

        for side, origin, ahead in sources(step):
            @pl.when(inside(origin))
            def _():
                owner = origin * 2 + core
                for q in range(naux):
                    band_other(owner, q).wait_recv()
                    pl.when(inside(ahead))(
                        lambda: band_on(owner, q, side, ahead * 2 + core).start()
                    )
                    band_other(owner, q).start()

    def relay_groups(step):
        for side, origin, ahead in sources(step):
            @pl.when(inside(origin))
            def _():
                owner = origin * 2 + core
                for part in range(2):
                    @pl.when(jnp.logical_not(carries(owner, part)))
                    def _():
                        coeff_other(owner, part).wait_recv()
                        coeff_other(owner, part).start()

        for side, origin, ahead in sources(step):
            @pl.when(inside(origin))
            def _():
                for part in range(2):
                    coeff_other(origin * 2 + 1 - core, part).wait_recv()

    def half_pair(origin):
        for j in range(2):
            owner = origin * 2 + j
            window = jnp.concatenate([coeffs[owner + near] for near in range(3)], axis=1)
            slab = jnp.concatenate([bands[owner, q] for q in range(naux)], axis=1)
            halves[j] = jnp.dot(window, slab, preferred_element_type=jnp.float32).astype(
                halves.dtype
            )

    def multiply(origin):
        total = None
        for q in range(naux):
            cut = slice(q * block, (q + 1) * block)
            both = jnp.concatenate([halves[0, :, cut], halves[1, :, cut]], axis=1)
            term = jnp.dot(own_t[cut, :], both, preferred_element_type=jnp.float32)
            total = term if total is None else total + term
        parts[origin] = total
        pl.when(origin != group)(lambda: part_out(origin).start())

    relay_row(1)
    for part in range(2):
        coeff_other(other, part).wait_recv()
    for q in range(naux):
        band_other(other, q).wait_recv()
    if chips > 2:
        relay_row(2)
    relay_groups(1)
    half_pair(chip)
    if chips > 3:
        relay_row(3)
    own_t[...] = halves[core].T
    multiply(chip)

    def forward(step, carry):
        pl.when(step + 3 < chips)(lambda: relay_row(step + 3))
        pl.when(step + 1 < chips)(lambda: relay_groups(step + 1))

        for side, origin, ahead in sources(step):
            @pl.when(inside(origin))
            def _():
                for q in range(naux):
                    band_other(origin * 2 + 1 - core, q).wait_recv()
                half_pair(origin)
                multiply(origin)

        return carry

    lax.fori_loop(1, chips, forward, 0)

    total = parts[group]
    for shift in range(1, groups):
        giver = lax.rem(group + shift, groups)
        send(parts.at[giver], arrived.at[giver], k_send.at[giver], k_recv.at[giver],
             {"aux": giver}).wait_recv()
        total = total + arrived[giver]
    for j in range(2):
        kept = kept_pairs[row, group * 2 + j].astype(jnp.float32)
        out_ref[:, j * block:(j + 1) * block] = total[:, j * block:(j + 1) * block] * kept

    def left_own(side, target):
        for part in range(2):
            pl.when(carries(row, part))(
                lambda part=part: coeff_on(row, part, side, target).wait_send()
            )
        for q in range(naux):
            band_on(row, q, side, target).wait_send()

    each_side(left_own)
    for part in range(2):
        coeff_other(row, part).wait_send()
    for q in range(naux):
        band_other(row, q).wait_send()

    def left(step, carry):
        for side, origin, ahead in sources(step):
            @pl.when(inside(origin))
            def _():
                owner = origin * 2 + core
                for part in range(2):
                    @pl.when(carries(owner, part))
                    def _():
                        pl.when(inside(ahead))(
                            lambda: coeff_on(owner, part, side, ahead * 2 + core).wait_send()
                        )
                        for shift in range(1, groups):
                            coeff_aux(owner, part, shift).wait_send()

                    coeff_other(owner, part).wait_send()
                for q in range(naux):
                    pl.when(inside(ahead))(
                        lambda: band_on(owner, q, side, ahead * 2 + core).wait_send()
                    )
                    band_other(owner, q).wait_send()

        return carry

    lax.fori_loop(1, chips, left, 0)
    for shift in range(1, groups):
        part_out(lax.rem(group + shift, groups)).wait_send()


def on_device(rows, groups, coeff, band, pairs):
    occupied, block = coeff.shape
    naux, depth, _ = band.shape
    chips = rows // 2
    dma = pltpu.SemaphoreType.DMA
    held = pl.BlockSpec(memory_space=pl.ANY)
    vmem = pl.BlockSpec(memory_space=pltpu.VMEM)
    flops = 2 * rows * naux * occupied * block * (depth + block)
    return pl.pallas_call(
        functools.partial(exchange_kernel, rows, groups),
        out_shape=jax.ShapeDtypeStruct((block, 2 * block), jnp.float32),
        in_specs=[held, held, held],
        out_specs=vmem,
        scratch_shapes=[
            pltpu.VMEM((rows + 2, occupied, block), jnp.bfloat16),
            pltpu.VMEM((rows, naux, depth, block), jnp.bfloat16),
            pltpu.VMEM((2, occupied, naux * block), jnp.bfloat16),
            pltpu.VMEM((naux * block, occupied), jnp.bfloat16),
            pltpu.VMEM((groups, block, 2 * block), jnp.float32),
            pltpu.VMEM((groups, block, 2 * block), jnp.float32),
            dma((2, rows, 2)), dma((rows, 2)), dma((chips, 2, groups - 1)), dma((rows, 2)),
            dma((2, rows, naux)), dma((rows, naux)), dma((rows, naux)),
            dma((groups,)), dma((groups,)), dma((3,)),
            pltpu.SMEM((rows, rows), jnp.int32),
        ],
        compiler_params=pltpu.CompilerParams(
            collective_id=0, has_side_effects=True, vmem_limit_bytes=48 * 2**20
        ),
        cost_estimate=pl.CostEstimate(flops=flops, bytes_accessed=2**20, transcendentals=0),
    )(coeff, band, pairs)


def solution(mesh):
    rows, groups = mesh.shape["row"], mesh.shape["aux"]
    placed = (P(None, "row"), P("aux", None, "row"), P())
    return jax.shard_map(
        functools.partial(on_device, rows, groups),
        mesh=mesh, in_specs=placed, out_specs=P("row", "aux"), check_vma=False,
    )
```
